32 devices in a mesh: width: 4 (over y, x), seq: 8 (over z, core).
Axes of the slice: x: 2, y: 2, z: 4, core: 2. Of those that a mesh axis runs over, the one named last changes fastest.
Arguments:
- activations: bfloat16 [8192, 28672], P('seq', 'width'), may hold values from -6 to 6
- errors: bfloat16 [8192, 8192], P('seq', 'width'), may hold values from -6 to 6
- proj_acts: bfloat16 [28672, 128], P('width'), may hold values from -0.03125 to 0.03125
- proj_errs: bfloat16 [8192, 128], P('width'), may hold values from -0.0625 to 0.0625
- fisher: float32 [16384, 16384], P('seq', 'width'), may hold values from -1 to 4, as said below
- queries: float32 [8, 2048, 128], P('seq', 'width'), may hold values from -6 to 6
Outputs:
- solution: float32 [8, 2048, 128], P('seq', 'width')
- residual: float32 [8, 2048, 128], P('seq', 'width')
- scores: float32 [128, 128], P(('width', 'seq'))
The draws below stay inside these ranges and needn't reach their ends.
Inputs may be any that keep to these rules, and one draw needn't show every extreme that they name: `fisher`: symmetric and positive definite.
All inputs are finite; a program needn't handle non-finite values.
Results may differ from the reference program's by a relative error of at most 0.003.
Values may be sent and summed in bfloat16 or wider, within the bound.
No kernel may reach another device: no remote copies, remote signals or barrier semaphores. Data moves between devices by JAX's collectives and lax.ppermute only.
A program may use at most 192 MiB of HBM per device.

```python
import math
import jax
import jax.numpy as jnp
from jax import lax

DA = 28672
DG = 8192
RANK = 128
SEQ_LEN = 64
QUERIES = 128
SEQS = 128
TOKENS = 8192
ENTRIES = 16384
N_SEQ = 8


def draw_fisher(key, part):
    key_diag = jax.random.fold_in(key, 11)
    key_off = jax.random.fold_in(key, 23)
    order = ENTRIES
    diag_values = jax.random.uniform(key_diag, (order,), jnp.float32, 2.0, 3.0)
    spread = jnp.clip(jax.random.normal(key_off, (order, order), jnp.float32), -6.0, 6.0)
    symmetric = (spread + spread.T) * (0.6 / (math.sqrt(2.0) * math.sqrt(order)))
    diag_index = jnp.arange(order)
    return symmetric.at[diag_index, diag_index].add(diag_values)


def steps_of(stream_key, shape, pieces, smallest, high):
    loudness, own = 1.0, jax.random.fold_in(stream_key, 6)
    for dim, parts in pieces:
        draws = jnp.exp(jax.random.uniform(jax.random.fold_in(own, dim), (parts,), jnp.float32, smallest / len(pieces), high / len(pieces)))
        loudness = loudness * jnp.repeat(draws, shape[dim] // parts).reshape([-1 if axis == dim else 1 for axis in range(len(shape))])
    return loudness


def normal_values(key, extent, scale, reach, split=(), held_as=jnp.bfloat16):
    entries = scale * jax.random.normal(key, extent, jnp.float32)
    if split:
        entries = entries * steps_of(key, extent, split, -0.22, 0.18)
    return jnp.clip(entries, -reach, reach).astype(held_as)


def setup_inputs(seed: int = 0) -> dict:
    keys = jax.random.split(jax.random.key(seed), 7)
    return {
        "activations": normal_values(keys[0], (TOKENS, DA), 1.0, 6.0, ((0, 8), (1, 4))),
        "errors": normal_values(keys[1], (TOKENS, DG), 1.0, 6.0, ((0, 8), (1, 4))),
        "proj_acts": normal_values(keys[2], (DA, RANK), DA ** -0.5, 0.03125, ((0, 4),)),
        "proj_errs": normal_values(keys[3], (DG, RANK), DG ** -0.5, 0.0625, ((0, 4),)),
        "fisher": draw_fisher(jax.random.fold_in(keys[6], 71), 0),
        "queries": normal_values(keys[5], (N_SEQ, ENTRIES // N_SEQ, QUERIES), 1.0, 6.0, ((0, 8), (1, 4)), jnp.float32),
    }


ridge_damp = 0.1
bound_low = 0.5
bound_high = 6.0


def chebyshev(apply_op, rhs):
    center = 0.5 * (bound_high + bound_low)
    half_width = 0.5 * (bound_high - bound_low)
    sigma_ratio = center / half_width
    rho_first = 1.0 / sigma_ratio
    rho_second = 1.0 / (2.0 * sigma_ratio - rho_first)
    step_one = rhs / center
    residue = rhs - apply_op(step_one)
    step_two = (rho_second * rho_first) * step_one + (2.0 * rho_second / half_width) * residue
    iterate = step_one + step_two
    residue = residue - apply_op(step_two)
    return iterate, residue


def reference(activations, errors, proj_acts, proj_errs, fisher, queries):
    highest = lax.Precision.HIGHEST
    act_proj = jnp.dot(activations, proj_acts, preferred_element_type=jnp.float32).reshape(SEQS, SEQ_LEN, RANK)
    err_proj = jnp.dot(errors, proj_errs, preferred_element_type=jnp.float32).reshape(SEQS, SEQ_LEN, RANK)
    seq_grads = (jnp.einsum("sti,stk->sik", err_proj, act_proj, precision=highest) / SEQ_LEN)
    seq_grads = seq_grads.reshape(SEQS, ENTRIES).astype(jnp.bfloat16)
    gram_sum = lax.dot_general(seq_grads, seq_grads, (((0,), (0,)), ((), ())), preferred_element_type=jnp.float32)
    diag_index = jnp.arange(ENTRIES)
    damped = (fisher + gram_sum / SEQS).at[diag_index, diag_index].add(ridge_damp)
    rhs = queries.reshape(ENTRIES, QUERIES)

    def apply_op(vector):
        return jnp.dot(damped, vector, precision=highest, preferred_element_type=jnp.float32)

    solution, residual = chebyshev(apply_op, rhs)
    scores = jnp.dot(seq_grads.astype(jnp.float32), solution, precision=highest, preferred_element_type=jnp.float32)
    return (solution.reshape(N_SEQ, ENTRIES // N_SEQ, QUERIES), residual.reshape(N_SEQ, ENTRIES // N_SEQ, QUERIES), scores)
```

```python
import jax
import jax.numpy as jnp
from jax import lax
from jax.experimental import pallas as pl
from jax.experimental.pallas import tpu as pltpu
from jax.sharding import PartitionSpec as P

SEQ_LEN = 64

ridge_damp = 0.1
bound_low = 0.5
bound_high = 6.0
center = 0.5 * (bound_high + bound_low)
half_width = 0.5 * (bound_high - bound_low)
rho_first = half_width / center
rho_second = 1.0 / (2.0 * center / half_width - rho_first)
fall = rho_second * rho_first
lead = (1.0 + fall) / center
tail = 2.0 * rho_second / half_width / center

BF16 = jnp.bfloat16
F32 = jnp.float32
HIGHEST = lax.Precision.HIGHEST
MIB = 1024 * 1024
NN = (((1,), (0,)), ((), ()))
NT = (((1,), (1,)), ((), ()))
TN = (((0,), (0,)), ((), ()))

WHOLE = pl.BlockSpec(memory_space=pltpu.VMEM)
SCALARS = pl.BlockSpec(memory_space=pltpu.SMEM)


def shaped(shape, dtype):
    return jax.ShapeDtypeStruct(shape, dtype)


def dot(a, b, dims, precision=None):
    return lax.dot_general(a, b, dims, precision=precision, preferred_element_type=F32)


def swap(x, axis, k):
    return lax.ppermute(x, axis, [(i, i ^ k) for i in range(lax.axis_size(axis))])


def call(body, out, args, flops=0, limit=32, **kw):
    moved = sum(a.size * a.dtype.itemsize for a in args)
    return pl.pallas_call(
        body,
        out_shape=out,
        compiler_params=pltpu.CompilerParams(vmem_limit_bytes=limit * MIB),
        cost_estimate=pl.CostEstimate(flops=flops, bytes_accessed=moved, transcendentals=0),
        **kw,
    )(*args)


def project(ranks, activations, errors, proj_acts, proj_errs, n_w):
    tokens, feats_a = activations.shape
    feats_e = errors.shape[1]
    rank = proj_acts.shape[1]
    own = tokens // n_w
    rows = min(128, own)
    per = own // rows

    def body(ranks_ref, act_ref, err_ref, pa_ref, pe_ref, *outs):
        step = pl.program_id(0)
        a = dot(act_ref[...], pa_ref[...], NN)
        e = dot(err_ref[...], pe_ref[...], NN)
        at = pl.multiple_of((step % per) * rows, rows)
        for r in range(n_w):

            @pl.when(step // per == r)
            def _():
                outs[r][pl.ds(at, rows), :rank] = a
                outs[r][pl.ds(at, rows), rank:] = e

    block = lambda i, ranks: ((ranks[0] ^ (i // per)) * per + i % per, 0)
    keep = lambda i, ranks: (0, 0)
    return pl.pallas_call(
        body,
        out_shape=[shaped((own, 2 * rank), F32)] * n_w,
        grid_spec=pltpu.PrefetchScalarGridSpec(
            num_scalar_prefetch=1,
            grid=(n_w * per,),
            in_specs=[
                pl.BlockSpec((rows, feats_a), block),
                pl.BlockSpec((rows, feats_e), block),
                pl.BlockSpec((feats_a, rank), keep),
                pl.BlockSpec((feats_e, rank), keep),
            ],
            out_specs=[pl.BlockSpec((own, 2 * rank), keep)] * n_w,
        ),
        compiler_params=pltpu.CompilerParams(vmem_limit_bytes=32 * MIB),
        cost_estimate=pl.CostEstimate(
            flops=2 * tokens * (feats_a + feats_e) * rank,
            bytes_accessed=2 * tokens * (feats_a + feats_e),
            transcendentals=0,
        ),
    )(ranks, activations, errors, proj_acts, proj_errs)


def gradients(parts):
    tokens, both = parts[0].shape
    rank = both // 2
    seqs = tokens // SEQ_LEN

    def body(*refs):
        ins, out = refs[:-1], refs[-1]
        total = ins[0][...]
        for ref in ins[1:]:
            total = total + ref[...]
        for j in range(seqs):
            rows = slice(j * SEQ_LEN, (j + 1) * SEQ_LEN)
            g = dot(total[rows, rank:], total[rows, :rank], TN, HIGHEST)
            out[j] = (g / SEQ_LEN).astype(BF16)

    return call(body, shaped((seqs, rank, rank), BF16), parts)


def first_product(ranks, fisher, rhs_t, n_w, n_s, parity):
    row_len, col_len = fisher.shape
    chunk = col_len // n_s
    count = rhs_t[0].shape[0]
    steps = n_s // 2
    width = min(256, chunk)
    sub = chunk // width
    shift = ridge_damp - center

    def body(ranks_ref, fisher_ref, *refs):
        vec, (y_ref, keep_ref) = refs[:n_w], refs[n_w:]
        t = pl.program_id(0) // sub
        h = pl.program_id(0) % sub
        w, s = ranks_ref[0], ranks_ref[1]
        p = 2 * t + parity
        cols = pl.ds(pl.multiple_of(h * width, width), width)
        total = jnp.zeros((count, width), F32)
        for r in range(n_w):
            rows = pl.ds(pl.multiple_of((w ^ r) * chunk, chunk), chunk)
            keep_ref[t, r, :, cols] = fisher_ref[rows, :].astype(BF16)

            @pl.when(w * n_s + (s ^ p) == s * n_w + (w ^ r))
            def _():
                i = lax.broadcasted_iota(jnp.int32, (chunk, width), 0)
                j = lax.broadcasted_iota(jnp.int32, (chunk, width), 1) + h * width
                block = fisher_ref[rows, :]
                keep_ref[t, r, :, cols] = (block + jnp.where(i == j, shift, 0.0)).astype(BF16)

            total = total + dot(vec[r][...], keep_ref[t, r, :, cols], NN)
        y_ref[t, :, cols] = total

    column = lambda i, ranks: (0, (ranks[1] ^ (2 * (i // sub) + parity)) * sub + i % sub)
    return pl.pallas_call(
        body,
        out_shape=[
            shaped((steps, count, chunk), F32),
            pltpu.VMEM((steps, n_w, chunk, chunk), BF16),
        ],
        grid_spec=pltpu.PrefetchScalarGridSpec(
            num_scalar_prefetch=1,
            grid=(steps * sub,),
            in_specs=[pl.BlockSpec((row_len, width), column)] + [WHOLE] * n_w,
            out_specs=[WHOLE, WHOLE],
        ),
        compiler_params=pltpu.CompilerParams(vmem_limit_bytes=24 * MIB),
        cost_estimate=pl.CostEstimate(
            flops=row_len * col_len * count,
            bytes_accessed=2 * row_len * col_len,
            transcendentals=0,
        ),
    )(ranks, fisher, *rhs_t)


def fold_cores(mine, theirs):
    steps, count, chunk = mine.shape

    def body(mine_ref, theirs_ref, own_ref, *outs):
        own_ref[...] = mine_ref[0] + theirs_ref[0]
        for t in range(1, steps):
            outs[t - 1][...] = (mine_ref[t] + theirs_ref[t]).astype(BF16)

    outs = [shaped((count, chunk), F32)] + [shaped((count, chunk), BF16)] * (steps - 1)
    return call(body, outs, [mine, theirs])


def fold_chips(own, others):
    def body(*refs):
        total = refs[0][...]
        for ref in refs[1:-1]:
            total = total + ref[...].astype(F32)
        refs[-1][...] = total.astype(BF16)

    return call(body, shaped(own.shape, BF16), [own, *others])


def panel(ranks, near, far, q_near, q_far, n_s):
    lines, group, rank = near[0].shape
    steps = len(near)
    seqs = n_s * group
    count, chunk = q_near[0].shape
    per = chunk // rank

    def body(ranks_ref, *refs):
        near_refs, far_ref = refs[:steps], refs[steps]
        q_refs, q_far_ref = refs[steps + 1 : 2 * steps + 1], refs[2 * steps + 1]
        g_ref, gq_ref = refs[2 * steps + 2 :]
        s = ranks_ref[1]
        total = jnp.zeros((seqs, count), F32)
        for p in range(n_s):
            for ii in range(per):
                line = (s ^ p) * per + ii
                for j in range(n_s):
                    piece = near_refs[j // 2][line] if j % 2 == 0 else far_ref[j // 2, line]
                    g_ref[p, j * group : (j + 1) * group, ii * rank : (ii + 1) * rank] = piece
            q = q_refs[p // 2][...] if p % 2 == 0 else q_far_ref[p // 2]
            total = total + dot(g_ref[p], q, NT)
        gq_ref[...] = total

    args = [ranks, *near, far, *q_near, q_far]
    return call(
        body,
        [shaped((n_s, seqs, chunk), BF16), shaped((seqs, count), F32)],
        args,
        in_specs=[SCALARS] + [WHOLE] * (len(args) - 1),
        out_specs=[WHOLE, WHOLE],
    )


def second_product(keep_even, keep_odd, y_near, y_far, grads):
    steps, n_w, chunk, _ = keep_even.shape
    n_s, seqs, _ = grads.shape
    count = y_near[0].shape[0]

    def body(even_ref, odd_ref, *refs):
        y_refs, y_far_ref, g_ref = refs[:steps], refs[steps], refs[steps + 1]
        tile_ref, small_ref, x_ref = refs[steps + 2 :]
        small = jnp.zeros((seqs, count + seqs), F32)
        for p in range(n_s):
            x_ref[p, :count] = y_refs[p // 2][...] if p % 2 == 0 else y_far_ref[p // 2]
            x_ref[p, count:] = g_ref[p]
            small = small + dot(g_ref[p], x_ref[p], NT)
        small_ref[...] = small

        def one(r, carry):
            total = jnp.zeros((chunk, count + seqs), F32)
            for p in range(n_s):
                block = even_ref[p // 2, r] if p % 2 == 0 else odd_ref[p // 2, r]
                total = total + dot(block, x_ref[p], NT)
            tile_ref[r] = total
            return carry

        lax.fori_loop(0, n_w, one, 0)

    args = [keep_even, keep_odd, *y_near, y_far, grads]
    return call(
        body,
        [shaped((n_w, chunk, count + seqs), F32), shaped((seqs, count + seqs), F32)],
        args,
        flops=2 * n_w * chunk * chunk * n_s * (count + seqs),
        in_specs=[WHOLE] * len(args),
        out_specs=[WHOLE, WHOLE],
        scratch_shapes=[pltpu.VMEM((n_s, count + seqs, chunk), BF16)],
    )


def combine(tile, small, first):
    n_w, chunk, both = tile.shape
    seqs, count = first.shape

    def body(tile_ref, small_ref, first_ref, own_ref, *outs):
        u = first_ref[...]
        for r in range(n_w):
            part = tile_ref[r, :, :count] + dot(tile_ref[r, :, count:], u, NN, HIGHEST)
            if r == 0:
                own_ref[...] = part
            else:
                outs[r - 1][...] = part.astype(BF16)
        outs[n_w - 1][...] = small_ref[:, :count] + dot(small_ref[:, count:], u, NN, HIGHEST)

    outs = [shaped((chunk, count), F32)] + [shaped((chunk, count), BF16)] * (n_w - 1)
    return call(body, outs + [shaped((seqs, count), F32)], [tile, small, first])


def finish(ranks, rhs, y_own, g_own, first, seconds, parts, n_w, n_s):
    chunk, count = rhs.shape
    seqs = first.shape[0]
    group = seqs // n_s
    local = seqs // (n_w * n_s)

    def body(ranks_ref, rhs_ref, y_ref, g_ref, first_ref, *refs):
        second_refs, part_refs = refs[:n_w], refs[n_w : 2 * n_w]
        sol_ref, res_ref, score_ref, coef_ref, order_ref = refs[2 * n_w :]
        w, s = ranks_ref[0], ranks_ref[1]
        source = (s * n_w + w) % n_s
        for p in range(n_s):
            rows = pl.ds(pl.multiple_of((source ^ s ^ p) * group, group), group)
            order_ref[p * group : (p + 1) * group, :] = g_ref[rows, :].astype(F32)
        first = first_ref[...]
        second = second_refs[0][...]
        for ref in second_refs[1:]:
            second = second + ref[...]
        second = second / seqs
        q = rhs_ref[...]
        g = order_ref[...]
        once = y_ref[...].astype(F32).T + dot(g, first, TN, HIGHEST)
        twice = part_refs[0][...] + dot(g, second, TN, HIGHEST)
        for ref in part_refs[1:]:
            twice = twice + ref[...].astype(F32)
        sol_ref[...] = lead * q - tail * once
        res_ref[...] = tail * twice - fall * q
        coef_ref[...] = seqs * (lead * first - tail * second)
        for j in range(local):
            row = (w * n_s + s) * local + j
            at = ((row // group) ^ s) * group + row % group
            score_ref[pl.ds(j, 1), :] = coef_ref[pl.ds(at, 1), :]

    args = [ranks, rhs, y_own, g_own, first, *seconds, *parts]
    return call(
        body,
        [shaped((chunk, count), F32), shaped((chunk, count), F32), shaped((local, count), F32)],
        args,
        in_specs=[SCALARS] + [WHOLE] * (len(args) - 1),
        out_specs=[WHOLE] * 3,
        scratch_shapes=[pltpu.VMEM((seqs, count), F32), pltpu.VMEM((seqs, chunk), F32)],
    )


def on_device(activations, errors, proj_acts, proj_errs, fisher, queries):
    n_w = lax.axis_size("width")
    n_s = lax.axis_size("seq")
    steps = n_s // 2
    ranks = jnp.stack([lax.axis_index("width"), lax.axis_index("seq")]).astype(jnp.int32)
    rank = proj_acts.shape[1]
    rhs = queries.reshape(queries.shape[1:])
    both = ("width", "seq")
    to_columns = []
    for block in range(n_w * n_s):
        by_row = (block % n_w) * n_s + block // n_w
        to_columns.append((by_row, block))
    to_rows = [(b, a) for a, b in to_columns]

    rhs_t = rhs.T.astype(BF16)
    rows_t = [rhs_t] + [swap(rhs_t, "width", r) for r in range(1, n_w)]
    q_cols = lax.ppermute(rhs_t, both, to_columns)
    q_near = [q_cols] + [swap(q_cols, "seq", 2 * t) for t in range(1, steps)]
    q_far = swap(jnp.stack(q_near), "seq", 1)

    pieces = project(ranks, activations, errors, proj_acts, proj_errs, n_w)
    pieces = [pieces[0]] + [swap(pieces[r], "width", r) for r in range(1, n_w)]
    grads = gradients(pieces)
    local = grads.shape[0]
    lines = rank // n_w
    split = grads.reshape(local, n_w, lines, rank).transpose(1, 0, 2, 3)
    split = lax.all_to_all(split, "width", split_axis=0, concat_axis=0, tiled=True)
    group = n_w * local
    near = split.reshape(group, lines, rank).transpose(1, 0, 2)
    near = [near] + [swap(near, "seq", 2 * t) for t in range(1, steps)]
    far = swap(jnp.stack(near), "seq", 1)
    grads, first = panel(ranks, near, far, q_near, q_far, n_s)
    g_own = lax.ppermute(grads[0], both, to_rows)
    seqs = first.shape[0]

    theirs, keep_odd = first_product(ranks, fisher, rows_t, n_w, n_s, 1)
    theirs = swap(theirs, "seq", 1)
    mine, keep_even = first_product(ranks, fisher, rows_t, n_w, n_s, 0)
    own, *sent = fold_cores(mine, theirs)
    y = fold_chips(own, [swap(sent[t - 1], "seq", 2 * t) for t in range(1, steps)])
    y_own = lax.ppermute(y, both, to_rows)
    y_near = [y] + [swap(y, "seq", 2 * t) for t in range(1, steps)]
    y_far = swap(jnp.stack(y_near), "seq", 1)

    first = sum([swap(first, "width", r) for r in range(1, n_w)], first) / seqs
    tile, small = second_product(keep_even, keep_odd, y_near, y_far, grads)
    own, *sent, second = combine(tile, small, first)
    parts = [own] + [swap(sent[r - 1], "width", r) for r in range(1, n_w)]
    seconds = [second] + [swap(second, "width", r) for r in range(1, n_w)]
    solution, residual, scores = finish(
        ranks, rhs, y_own, g_own, first, seconds, parts, n_w, n_s
    )
    return solution.reshape(queries.shape), residual.reshape(queries.shape), scores


def solution(mesh):
    placed = (
        P("seq", "width"),
        P("seq", "width"),
        P("width", None),
        P("width", None),
        P("seq", "width"),
        P("seq", "width", None),
    )
    return jax.shard_map(
        on_device,
        mesh=mesh,
        in_specs=placed,
        out_specs=(P("seq", "width", None), P("seq", "width", None), P(("width", "seq"), None)),
        check_vma=False,
    )
```

```python
import jax
import jax.numpy as jnp
from jax import lax
from jax.experimental import pallas as pl
from jax.experimental.pallas import tpu as pltpu
from jax.sharding import PartitionSpec as P

SEQ_LEN = 64

ridge_damp = 0.1
bound_low = 0.5
bound_high = 6.0
center = 0.5 * (bound_high + bound_low)
half_width = 0.5 * (bound_high - bound_low)
rho_first = half_width / center
rho_second = 1.0 / (2.0 * center / half_width - rho_first)
fall = rho_second * rho_first
lead = (1.0 + fall) / center
tail = 2.0 * rho_second / half_width / center

BF16 = jnp.bfloat16
F32 = jnp.float32
HIGHEST = lax.Precision.HIGHEST
MIB = 1024 * 1024
NN = (((1,), (0,)), ((), ()))
NT = (((1,), (1,)), ((), ()))
TN = (((0,), (0,)), ((), ()))

WHOLE = pl.BlockSpec(memory_space=pltpu.VMEM)
SCALARS = pl.BlockSpec(memory_space=pltpu.SMEM)


BRIEF = pl.CostEstimate(flops=1, bytes_accessed=1, transcendentals=0)


def shaped(shape, dtype):
    return jax.ShapeDtypeStruct(shape, dtype)


def dot(a, b, dims, precision=None):
    return lax.dot_general(a, b, dims, precision=precision, preferred_element_type=F32)


def swap(x, axis, k):
    return lax.ppermute(x, axis, [(i, i ^ k) for i in range(lax.axis_size(axis))])


def call(body, out, args, flops=0, limit=8, **kw):
    return pl.pallas_call(
        body,
        out_shape=out,
        compiler_params=pltpu.CompilerParams(vmem_limit_bytes=limit * MIB),
        cost_estimate=BRIEF,
        **kw,
    )(*args)


def project(ranks, activations, errors, proj_acts, proj_errs, n_w):
    tokens, feats_a = activations.shape
    feats_e = errors.shape[1]
    rank = proj_acts.shape[1]
    own = tokens // n_w
    rows = min(256, own)
    per = own // rows
    half = feats_a // 2
    order = [(r, h) for r in range(n_w - 1, -1, -1) for _ in range(per) for h in range(2)]
    depth = min(4, len(order))

    def body(ranks_ref, act_ref, err_ref, pa_ref, pe_ref, *refs):
        outs = refs[:n_w]
        pa, pe, act, err, wsems, sems = refs[n_w:]

        def copies(n):
            r, h = order[n]
            at = ((ranks_ref[0] ^ r) * per + n // 2 % per) * rows
            some = pl.ds(pl.multiple_of(at, rows), rows)
            slot = n % depth
            source = act_ref.at[some, h * half : (h + 1) * half]
            moves = [pltpu.make_async_copy(source, act.at[slot], sems.at[0, slot])]
            if h == 0:
                slot = n // 2 % 2
                moves.append(pltpu.make_async_copy(err_ref.at[some], err.at[slot], sems.at[1, slot]))
            return moves

        weights = (
            pltpu.make_async_copy(pa_ref, pa, wsems.at[0]),
            pltpu.make_async_copy(pe_ref, pe, wsems.at[1]),
        )
        for one in weights:
            one.start()
        for n in range(depth):
            for one in copies(n):
                one.start()
        for one in weights:
            one.wait()
        for n, (r, h) in enumerate(order):
            for one in copies(n):
                one.wait()
            some = slice((n // 2 % per) * rows, (n // 2 % per + 1) * rows)
            part = dot(act[n % depth], pa[h * half : (h + 1) * half], NN)
            if h == 0:
                outs[r][some, :rank] = part
                outs[r][some, rank:] = dot(err[n // 2 % 2], pe[...], NN)
            else:
                outs[r][some, :rank] += part
            if n + depth < len(order):
                for one in copies(n + depth):
                    one.start()

    return pl.pallas_call(
        body,
        out_shape=[shaped((own, 2 * rank), F32)] * n_w,
        in_specs=[SCALARS] + [pl.BlockSpec(memory_space=pl.ANY)] * 4,
        out_specs=[WHOLE] * n_w,
        scratch_shapes=[
            pltpu.VMEM(proj_acts.shape, BF16),
            pltpu.VMEM(proj_errs.shape, BF16),
            pltpu.VMEM((depth, rows, half), BF16),
            pltpu.VMEM((2, rows, feats_e), BF16),
            pltpu.SemaphoreType.DMA((2,)),
            pltpu.SemaphoreType.DMA((2, depth)),
        ],
        compiler_params=pltpu.CompilerParams(vmem_limit_bytes=18 * MIB),
        cost_estimate=BRIEF,
    )(ranks, activations, errors, proj_acts, proj_errs)


def gradients(ranks, parts):
    n_w = len(parts)
    tokens, both = parts[0].shape
    rank = both // 2
    seqs = tokens // SEQ_LEN
    lines = rank // n_w

    def body(ranks_ref, *refs):
        ins, outs, all_ref = refs[:n_w], refs[n_w : 2 * n_w], refs[2 * n_w]
        w = ranks_ref[0]
        total = ins[0][...]
        for ref in ins[1:]:
            total = total + ref[...]
        for j in range(seqs):
            rows = slice(j * SEQ_LEN, (j + 1) * SEQ_LEN)
            g = dot(total[rows, rank:], total[rows, :rank], TN, HIGHEST)
            all_ref[j] = (g / SEQ_LEN).astype(BF16)
        for r in range(n_w):
            some = pl.ds(pl.multiple_of((w ^ r) * lines, lines), lines)
            for j in range(seqs):
                outs[r][j] = all_ref[j, some, :]

    return call(
        body,
        [shaped((seqs, lines, rank), BF16)] * n_w,
        [ranks, *parts],
        limit=8,
        in_specs=[SCALARS] + [WHOLE] * n_w,
        out_specs=[WHOLE] * n_w,
        scratch_shapes=[pltpu.VMEM((seqs, rank, rank), BF16)],
    )


def join(ranks, pieces, mine, theirs):
    n_w = len(pieces)
    seqs, lines, rank = pieces[0].shape
    count, chunk = mine.shape[1:]
    group = n_w * seqs
    rows = lines * group
    blocks = chunk // rank

    def body(ranks_ref, *refs):
        ins, mine_ref, theirs_ref, out, order_ref = refs[:n_w], *refs[n_w:]
        for r in range(n_w):
            for j in range(seqs):
                order_ref[(ranks_ref[0] ^ r) * seqs + j] = ins[r][j].astype(F32)
        grads = jnp.swapaxes(order_ref[...], 0, 1).astype(BF16)
        out[:rows] = grads.reshape(rows, rank)
        total = (mine_ref[0] + theirs_ref[0].astype(F32)).astype(BF16)
        for b in range(blocks):
            out[rows + b * count : rows + (b + 1) * count] = total[:, b * rank : (b + 1) * rank]

    return call(
        body,
        shaped((rows + blocks * count, rank), BF16),
        [ranks, *pieces, mine, theirs],
        limit=8,
        in_specs=[SCALARS] + [WHOLE] * (n_w + 2),
        out_specs=WHOLE,
        scratch_shapes=[pltpu.VMEM((group, lines, rank), F32)],
    )


def first_product(ranks, fisher, rhs_t, n_w, n_s, parity):
    row_len, col_len = fisher.shape
    chunk = col_len // n_s
    count = rhs_t[0].shape[0]
    steps = n_s // 2
    shift = ridge_damp - center
    blocks = [(t, r) for t in range(steps) for r in range(n_w)]
    depth = min(8, len(blocks))

    def body(ranks_ref, fisher_ref, *refs):
        vec, (y_ref, keep_ref, held, sems) = refs[:n_w], refs[n_w:]
        w, s = ranks_ref[0], ranks_ref[1]

        def copy(n):
            t, r = blocks[n]
            rows = pl.ds(pl.multiple_of((w ^ r) * chunk, chunk), chunk)
            cols = pl.ds(pl.multiple_of((s ^ (2 * t + parity)) * chunk, chunk), chunk)
            slot = n % depth
            return pltpu.make_async_copy(fisher_ref.at[rows, cols], held.at[slot], sems.at[slot])

        for n in range(depth):
            copy(n).start()
        for n, (t, r) in enumerate(blocks):
            copy(n).wait()
            slot = n % depth
            keep_ref[t, r] = held[slot].astype(BF16)

            @pl.when(w * n_s + (s ^ (2 * t + parity)) == s * n_w + (w ^ r))
            def _():
                i = lax.broadcasted_iota(jnp.int32, (chunk, chunk), 0)
                j = lax.broadcasted_iota(jnp.int32, (chunk, chunk), 1)
                keep_ref[t, r] = (held[slot] + jnp.where(i == j, shift, 0.0)).astype(BF16)

            part = dot(vec[r][...], keep_ref[t, r], NN)
            if r == 0:
                y_ref[t] = part
            else:
                y_ref[t] += part
            if n + depth < len(blocks):
                copy(n + depth).start()

    return pl.pallas_call(
        body,
        out_shape=[
            shaped((steps, count, chunk), F32),
            pltpu.VMEM((steps, n_w, chunk, chunk), BF16),
        ],
        in_specs=[SCALARS, pl.BlockSpec(memory_space=pl.ANY)] + [WHOLE] * n_w,
        out_specs=[WHOLE, WHOLE],
        scratch_shapes=[
            pltpu.VMEM((depth, chunk, chunk), F32),
            pltpu.SemaphoreType.DMA((depth,)),
        ],
        compiler_params=pltpu.CompilerParams(vmem_limit_bytes=12 * MIB),
        cost_estimate=BRIEF,
    )(ranks, fisher, *rhs_t)


def fold(mine, theirs):
    left, count, chunk = mine.shape

    def body(mine_ref, theirs_ref, keep_ref, send_ref):
        for i in range(left):
            total = mine_ref[i] + theirs_ref[i].astype(F32)
            if i % 2 == 0:
                keep_ref[i // 2] = total
            else:
                send_ref[i // 2] = total.astype(BF16)

    half = (left // 2, count, chunk)
    return call(body, [shaped(half, F32), shaped(half, BF16)], [mine, theirs])


def halves(x):
    high = x.astype(BF16)
    return high, (x - high.astype(F32)).astype(BF16)


def panel(ranks, joined, rows_t, group):
    n_s = len(joined)
    n_w = len(rows_t)
    count, chunk = rows_t[0].shape
    rank = joined[0].shape[1]
    seqs = n_s * group
    per = chunk // rank
    rows = joined[0].shape[0] - per * count
    ratio = n_s // n_w

    def body(ranks_ref, *refs):
        in_refs, q_refs = refs[:n_s], refs[n_s : n_s + n_w]
        x_ref, both_ref, product_ref, out = refs[n_s + n_w :]
        w, s = ranks_ref[0], ranks_ref[1]
        both = jnp.zeros((seqs, count + seqs), F32)
        for p in range(n_s):
            for ii in range(per):
                lanes = slice(ii * rank, (ii + 1) * rank)
                x_ref[p, :count, lanes] = in_refs[p][rows + ii * count : rows + (ii + 1) * count]
                line = pl.ds(pl.multiple_of(((s ^ p) * per + ii) * group, group), group)
                for j in range(n_s):
                    at = pl.ds(pl.multiple_of(count + (s ^ j) * group, group), group)
                    x_ref[p, at, lanes] = in_refs[j][line, :]
            both = both + dot(x_ref[p, count:], x_ref[p], NT)
        both_ref[...] = both
        product = jnp.zeros((seqs, count), F32)
        for r in range(n_w):
            at = s ^ ((s % ratio) * n_w + (w ^ r))
            product = product + dot(x_ref[at, count:], q_refs[r][...], NT)
        product = jnp.where(s // ratio == w, product, 0.0)
        product_ref[...] = product
        out[0, :, : count + seqs], out[1, :, : count + seqs] = halves(both)
        out[0, :, count + seqs :], out[1, :, count + seqs :] = halves(product)

    args = [ranks, *joined, *rows_t]
    outs = [
        shaped((n_s, count + seqs, chunk), BF16),
        shaped((seqs, count + seqs), F32),
        shaped((seqs, count), F32),
        shaped((2, seqs, 2 * count + seqs), BF16),
    ]
    return call(
        body,
        outs,
        args,
        limit=12,
        in_specs=[SCALARS] + [WHOLE] * (len(args) - 1),
        out_specs=[WHOLE] * len(outs),
    )


def settle(both, product, others):
    wide = both.shape[1]

    def body(both_ref, product_ref, *refs):
        total, right = both_ref[...], product_ref[...]
        for ref in refs[:-2]:
            whole = ref[0].astype(F32) + ref[1].astype(F32)
            total = total + whole[:, :wide]
            right = right + whole[:, wide:]
        refs[-2][...] = total
        refs[-1][...] = right

    outs = [shaped(x.shape, F32) for x in (both, product)]
    return call(body, outs, [both, product, *others], limit=8)


def second_product(keep_even, keep_odd, x):
    _, n_w, chunk, _ = keep_even.shape
    n_s, wide, _ = x.shape

    def body(even_ref, odd_ref, x_ref, *outs):
        for r in range(n_w - 1, -1, -1):
            total = jnp.zeros((chunk, wide), F32)
            for p in range(n_s):
                block = even_ref[p // 2, r] if p % 2 == 0 else odd_ref[p // 2, r]
                total = total + dot(block, x_ref[p], NT)
            outs[r][...] = total.astype(outs[r].dtype)

    outs = [shaped((chunk, wide), F32)] + [shaped((chunk, wide), BF16)] * (n_w - 1)
    return call(
        body,
        outs,
        [keep_even, keep_odd, x],
        limit=12,
        in_specs=[WHOLE] * 3,
        out_specs=[WHOLE] * len(outs),
    )


def prepare(ranks, rhs, x_own, both, first, n_w, n_s):
    chunk, count = rhs.shape
    seqs = both.shape[0]
    local = seqs // (n_w * n_s)

    def body(ranks_ref, rhs_ref, x_ref, both_ref, first_in_ref, sol_ref, res_ref, score_ref, first_ref, coef_ref):
        w, s = ranks_ref[0], ranks_ref[1]
        first = first_in_ref[...] / seqs
        first_ref[...] = first
        second = both_ref[:, :count] + dot(both_ref[:, count:], first, NN, HIGHEST)
        second = second / seqs
        q = rhs_ref[...]
        g = x_ref[count:].astype(F32)
        once = x_ref[:count].astype(F32).T + dot(g, first, TN, HIGHEST)
        sol_ref[...] = lead * q - tail * once
        res_ref[...] = tail * dot(g, second, TN, HIGHEST) - fall * q
        coef_ref[...] = seqs * (lead * first - tail * second)
        for j in range(local):
            row = (w * n_s + s) * local + j
            score_ref[pl.ds(j, 1), :] = coef_ref[pl.ds(row, 1), :]

    args = [ranks, rhs, x_own, both, first]
    outs = [shaped((chunk, count), F32)] * 2
    outs += [shaped((local, count), F32), shaped((seqs, count), F32)]
    return call(
        body,
        outs,
        args,
        limit=8,
        in_specs=[SCALARS] + [WHOLE] * (len(args) - 1),
        out_specs=[WHOLE] * len(outs),
        scratch_shapes=[pltpu.VMEM((seqs, count), F32)],
    )


def finish(residual, first, own, others):
    count = residual.shape[1]

    def body(res_in_ref, first_ref, own_ref, *refs):
        total = own_ref[...]
        for ref in refs[:-1]:
            total = total + ref[...].astype(F32)
        total = total[:, :count] + dot(total[:, count:], first_ref[...], NN, HIGHEST)
        refs[-1][...] = res_in_ref[...] + tail * total

    return call(body, shaped(residual.shape, F32), [residual, first, own, *others], limit=8)


def turn(rhs):
    def body(rhs_ref, out_ref):
        out_ref[...] = rhs_ref[...].T.astype(BF16)

    return call(body, shaped(rhs.shape[::-1], BF16), [rhs], limit=8)


def on_device(activations, errors, proj_acts, proj_errs, fisher, queries):
    n_w = lax.axis_size("width")
    n_s = lax.axis_size("seq")
    ranks = jnp.stack([lax.axis_index("width"), lax.axis_index("seq")]).astype(jnp.int32)
    rhs = queries.reshape(queries.shape[1:])
    to_rows = [(b, (b % n_w) * n_s + b // n_w) for b in range(n_w * n_s)]

    rhs_t = turn(rhs)
    rows_t = [rhs_t] + [swap(rhs_t, "width", r) for r in range(1, n_w)]

    activations, errors, proj_acts, proj_errs, fisher = [
        pltpu.with_memory_space_constraint(x, pltpu.HBM)
        for x in (activations, errors, proj_acts, proj_errs, fisher)
    ]
    pieces = project(ranks, activations, errors, proj_acts, proj_errs, n_w)
    fisher, *pieces = lax.optimization_barrier((fisher, *pieces))
    pieces = [pieces[0]] + [swap(pieces[r], "width", r) for r in range(1, n_w)]

    theirs, keep_odd = first_product(ranks, fisher, rows_t, n_w, n_s, 1)
    theirs = swap(theirs, "seq", 1)
    mine, keep_even = first_product(ranks, fisher, rows_t, n_w, n_s, 0)
    keep, sent = fold(mine, theirs)
    sent = swap(sent, "seq", 2)
    keep, sent, *pieces = lax.optimization_barrier((keep, sent, *pieces))
    grads = gradients(ranks, pieces)
    group = n_w * grads[0].shape[0]
    bit = 4
    while keep.shape[0] > 1:
        keep, sent = fold(keep, sent)
        sent, *grads = lax.optimization_barrier((sent, *grads))
        sent = swap(sent, "seq", bit)
        bit *= 2
    grads = [grads[0]] + [swap(grads[r], "width", r) for r in range(1, n_w)]
    joined = {0: join(ranks, grads, keep, sent)}
    bit = n_s // 2
    while bit:
        joined |= {p | bit: swap(joined[p], "seq", bit) for p in list(joined)}
        bit //= 2
    joined = [joined[p] for p in range(n_s)]

    x, both, product, sent = panel(ranks, joined, rows_t, group)
    small = [swap(sent, "width", r) for r in range(1, n_w)]
    x_own = lax.ppermute(x[0], ("width", "seq"), to_rows)
    own, *sent = second_product(keep_even, keep_odd, x)
    sent = [swap(sent[r - 1], "width", r) for r in range(1, n_w)]
    x_own, *small = lax.optimization_barrier((x_own, *small))
    both, product = settle(both, product, small)
    bit = 1
    while bit < n_s:
        product = product + swap(product, "seq", bit)
        bit *= 2
    solution, residual, scores, first = prepare(ranks, rhs, x_own, both, product, n_w, n_s)
    residual = finish(residual, first, own, sent)
    return solution.reshape(queries.shape), residual.reshape(queries.shape), scores


def solution(mesh):
    placed = (
        P("seq", "width"),
        P("seq", "width"),
        P("width", None),
        P("width", None),
        P("seq", "width"),
        P("seq", "width", None),
    )
    return jax.shard_map(
        on_device,
        mesh=mesh,
        in_specs=placed,
        out_specs=(P("seq", "width", None), P("seq", "width", None), P(("width", "seq"), None)),
        check_vma=False,
    )
```
